256 devices in a mesh: particle: 16 (over x_hi, z), shard: 16 (over y, x_lo, core).
Axes of the slice: x: 4 (x_hi: 2, x_lo: 2; x = x_hi * 2 + x_lo), y: 4, z: 8, core: 2. Of those that a mesh axis runs over, the one named last changes fastest.
Arguments:
- hidden: bfloat16 [32, 1024, 2432], P('particle', 'shard'), may hold values from -6 to 6
- ancestors: int32 [32], replicated, may hold values from 0 to 31
- timestep: int32 [1], replicated, may hold values from 0 to 27
- mod_table: float32 [28, 3, 2432], replicated, may hold values from -4 to 4
- w_qkv: bfloat16 [2432, 3648], P('shard'), may hold values from -0.125 to 0.125
- w_out: bfloat16 [1216, 2432], P('shard'), may hold values from -0.15625 to 0.15625
- q_gain: float32 [64], replicated, may hold values from 0.7 to 12
- k_gain: float32 [64], replicated, may hold values from 0.7 to 12
- text_kv: bfloat16 [2, 333, 1216], replicated, may hold values from -6 to 6
Outputs:
- block_out: bfloat16 [32, 1024, 2432], P('particle', 'shard')
The draws below stay inside these ranges and needn't reach their ends.
All inputs are finite; a program needn't handle non-finite values.
Results may differ from the reference program's by a relative error of at most 0.014.
The reference program's roundings to bfloat16 on the way (of `picked`, `modulated`, `probs` and `attended`) count: a program that leaves them out, or rounds other values in their place, can miss the bound.
Values may be sent and summed in bfloat16 or wider, within the bound.
No kernel may reach another device: no remote copies, remote signals or barrier semaphores. Data moves between devices by JAX's collectives and lax.ppermute only.
A program may use at most 128 MiB of HBM per device.

```python
import math
import jax
import jax.numpy as jnp
from jax import lax

D = 2432
HD = 64
HEADS = 19
TXT = 333
STEPS = 28
PARTICLES = 32
IMG = 1024


def gain_values(key, low, high):
    spread = jax.random.uniform(key, (HD,), jnp.float32, math.log(low), math.log(high))
    return jnp.exp(spread)


def draw_q_gain(key, part):
    key = jax.random.fold_in(key, 5)
    gains = gain_values(key, 0.7, 2.5)
    return gains.astype(jnp.float32)


def draw_k_gain(key, part):
    key = jax.random.fold_in(key, 9)
    gains = gain_values(key, 0.7, 2.5)
    return gains.astype(jnp.float32)


def place_ends(result, rng, smallest, high):
    index_at = [jax.random.randint(jax.random.fold_in(rng, axis), (), 0, length) for axis, length in enumerate(result.shape)]
    longest = result.shape.index(max(result.shape))
    neighbour = index_at[:longest] + [(index_at[longest] + 1) % result.shape[longest]] + index_at[longest + 1:]
    return result.at[tuple(index_at)].set(smallest).at[tuple(neighbour)].set(high)


def level_of(key, extent, cuts, smallest, largest):
    level = 1.0
    for axis_at, blocks in cuts:
        draws = jax.random.uniform(jax.random.fold_in(jax.random.fold_in(key, 6), axis_at), (blocks,), jnp.float32, smallest / len(cuts), largest / len(cuts))
        level = level * jnp.repeat(jnp.exp(draws), extent[axis_at] // blocks).reshape((-1,) + (1,) * (len(extent) - 1 - axis_at))
    return level


def bell_draw(stream_key, extent, width, bound, split=(), dtype=jnp.bfloat16):
    values = width * jax.random.normal(stream_key, extent, jnp.float32)
    if split:
        values = values * level_of(stream_key, extent, split, -0.22, 0.18)
    return jnp.clip(values, -bound, bound).astype(dtype)


def setup_inputs(seed: int = 0) -> dict:
    splits = jax.random.split(jax.random.key(seed), 10)
    hidden = bell_draw(splits[0], (PARTICLES, IMG, D), 1.0, 6.0, ((0, 16), (1, 16)))
    ancestors = place_ends(jax.random.randint(splits[1], (PARTICLES,), 0, PARTICLES), jax.random.fold_in(splits[1], 1), 0, PARTICLES - 1).astype(jnp.int32)
    timestep = jax.random.randint(splits[2], (1,), 0, STEPS).astype(jnp.int32)
    mod_table = bell_draw(splits[3], (STEPS, 3, D), 1.0, 4.0, (), jnp.float32)
    w_qkv = bell_draw(splits[4], (D, 3 * HEADS * HD), D ** -0.5, 0.125, ((0, 16),))
    w_out = bell_draw(splits[5], (HEADS * HD, D), (HEADS * HD) ** -0.5, 0.15625, ((0, 16),))
    q_gain = draw_q_gain(jax.random.fold_in(splits[9], 71), 0)
    k_gain = draw_k_gain(jax.random.fold_in(splits[9], 71), 0)
    text_kv = bell_draw(splits[8], (2, TXT, HEADS * HD), 1.0, 6.0)
    return dict(hidden=hidden, ancestors=ancestors, timestep=timestep, mod_table=mod_table, w_qkv=w_qkv, w_out=w_out, q_gain=q_gain, k_gain=k_gain, text_kv=text_kv)


def head_norm(values, gain):
    squares = lax.optimization_barrier(jnp.mean(values * values, axis=-1, keepdims=True))
    return (values * lax.rsqrt(squares + 1e-06) * gain).astype(jnp.bfloat16)

def reference(hidden, ancestors, timestep, mod_table, w_qkv, w_out, q_gain, k_gain, text_kv):
    picked = jnp.take(hidden, ancestors, axis=0)
    modulation = lax.dynamic_index_in_dim(mod_table, timestep[0], 0, keepdims=False)
    shift_row = modulation[0]
    scale_row = modulation[1]
    gate_row = modulation[2]
    inner = w_out.shape[0]
    heads = inner // HD
    text_keys = text_kv[0].reshape(TXT, heads, HD).astype(jnp.float32)
    text_values = text_kv[1].reshape(TXT, heads, HD).astype(jnp.float32)

    def one_particle(state):
        floats = state.astype(jnp.float32)
        center = lax.optimization_barrier(jnp.mean(floats, axis=-1, keepdims=True))
        spread = lax.optimization_barrier(jnp.mean((floats - center) ** 2, axis=-1, keepdims=True))
        normed = (floats - center) * lax.rsqrt(spread + 1e-06)
        modulated = (normed * (1.0 + scale_row) + shift_row).astype(jnp.bfloat16)
        qkv = jnp.dot(modulated, w_qkv, preferred_element_type=jnp.float32)
        query = head_norm(qkv[:, :inner].reshape(-1, heads, HD), q_gain)
        keys = head_norm(qkv[:, inner:2 * inner].reshape(-1, heads, HD), k_gain)
        values = qkv[:, 2 * inner:].reshape(-1, heads, HD).astype(jnp.bfloat16)
        all_keys = jnp.concatenate([keys.astype(jnp.float32), text_keys], axis=0)
        all_values = jnp.concatenate([values.astype(jnp.float32), text_values], axis=0)
        scores = jnp.einsum('rhd,khd->hrk', query.astype(jnp.float32), all_keys) * (1.0 / jnp.sqrt(jnp.float32(HD)))
        highest = lax.optimization_barrier(jnp.max(scores, axis=-1, keepdims=True))
        powers = jnp.exp(scores - highest)
        totals = lax.optimization_barrier(jnp.sum(powers, axis=-1))
        probs = powers.astype(jnp.bfloat16).astype(jnp.float32)
        mixed = jnp.einsum('hrk,khd->hrd', probs, all_values) / totals[:, :, None]
        attended = jnp.transpose(mixed, (1, 0, 2)).reshape(-1, inner).astype(jnp.bfloat16)
        projected = jnp.dot(attended, w_out, preferred_element_type=jnp.float32)
        return (floats + gate_row * projected).astype(jnp.bfloat16)
    return lax.map(one_particle, picked)
```

```python
import functools

import jax
import jax.numpy as jnp
import numpy as np
from jax import lax
from jax.experimental import pallas as pl
from jax.experimental.pallas import tpu as pltpu
from jax.sharding import Mesh, PartitionSpec as P

HD = 64
AXES = ("xh", "z", "y", "xl", "c")
SIZES = (2, 8, 4, 2, 2)
GROUP = ("xh", "z")
GROUPS = 16
Y = 4
G = 4
NH = 5
HC = NH * HD
RT = 16


def params(mib=16):
    return pltpu.CompilerParams(vmem_limit_bytes=mib * 1024 * 1024)


def whole():
    return pl.BlockSpec(memory_space=pltpu.VMEM)


def scalar():
    return pl.BlockSpec(memory_space=pltpu.SMEM)


def swap(x, axis):
    return lax.ppermute(x, axis, [(0, 1), (1, 0)])


def turn(x, axis, by):
    n = SIZES[AXES.index(axis)]
    return lax.ppermute(x, axis, [(i, (i + by) % n) for i in range(n)])


def pack_kernel(fw, x_ref, o_ref):
    parts, rows, _ = x_ref.shape
    bw = o_ref.shape[-1] // Y
    for p in range(parts):
        for i in range(rows // RT):
            for g in range(G):
                pieces = []
                for y in range(Y):
                    lo = (y * G + g) * fw
                    pieces.append(x_ref[p, i * RT : (i + 1) * RT, lo : lo + fw])
                    pieces.append(jnp.zeros((RT, bw - fw), x_ref.dtype))
                o_ref[G * i + g, p] = jnp.concatenate(pieces, axis=-1)


def restore_kernel(fw, x_ref, o_ref):
    parts, rows, _ = o_ref.shape
    bw = x_ref.shape[-1] // Y
    for p in range(parts):
        for i in range(rows // RT):
            row = [x_ref[G * i + g, p] for g in range(G)]
            pieces = [row[g][:, y * bw : y * bw + fw] for y in range(Y) for g in range(G)]
            o_ref[p, i * RT : (i + 1) * RT, :] = jnp.concatenate(pieces, axis=-1)


def pick_kernel(a_ref, x_ref, o_ref):
    def step(p, _):
        o_ref[p] = x_ref[a_ref[p]]
        return 0

    lax.fori_loop(0, x_ref.shape[0], step, 0, unroll=4)


def norm_kernel(width, s_ref, x_ref, m_ref, k_ref, keep_ref, send_ref):
    parts = x_ref.shape[1]
    count = keep_ref.shape[1] // RT
    side = s_ref[0]
    live = k_ref[...]
    for which, o_ref in enumerate((keep_ref, send_ref)):
        for i in range(count):
            floats = [x_ref[G * i + g, side ^ which].astype(jnp.float32) for g in range(G)]
            center = sum(jnp.sum(f, axis=-1, keepdims=True) for f in floats) / width
            moved = [(f - center) * live for f in floats]
            spread = sum(jnp.sum(m * m, axis=-1, keepdims=True) for m in moved) / width
            inverse = lax.rsqrt(spread + 1e-06)
            for g in range(G):
                out = (moved[g] * inverse) * (1.0 + m_ref[1, g : g + 1]) + m_ref[0, g : g + 1]
                o_ref[g, i * RT : (i + 1) * RT, :] = out.astype(jnp.bfloat16)


def weight_kernel(s_ref, w_ref, o_ref):
    inner = w_ref.shape[1] // 3
    for y in range(Y):
        at = (y - s_ref[0]) & 3
        pieces = []
        for t in range(3):
            lo, hi = y * HC, min(inner, (y + 1) * HC)
            pieces.append(w_ref[:, t * inner + lo : t * inner + hi])
            if hi - lo < HC:
                pieces.append(jnp.zeros((w_ref.shape[0], HC - hi + lo), w_ref.dtype))
        o_ref[at] = jnp.concatenate(pieces, axis=-1)


def place_kernel(order, s_ref, *refs):
    *pieces, o_ref = refs
    for k, piece in enumerate(pieces):
        o_ref[order(k, s_ref)] = piece[...]


def placed_in_order(order, scalars, pieces):
    count = len(pieces)
    return pl.pallas_call(
        functools.partial(place_kernel, order),
        out_shape=jax.ShapeDtypeStruct((count,) + pieces[0].shape, pieces[0].dtype),
        in_specs=[scalar()] + [whole()] * count,
        out_specs=whole(),
        compiler_params=params(),
    )(scalars, *pieces)


def qkv_kernel(s_ref, *refs):
    x_refs, w_refs = refs[:4], refs[4:8]
    qg_ref, kg_ref, q_ref, kv_ref, x_buf, w_buf, sems = refs[8:]
    own = s_ref[0]
    rows, gw = x_refs[0].shape[1:]
    copies = [
        pltpu.make_async_copy(w_ref, w_buf.at[own ^ flip], sems.at[flip])
        for flip, w_ref in enumerate(w_refs)
    ]
    for copy in copies:
        copy.start()
    for k, x_ref in enumerate(x_refs):
        for g in range(G):
            x_buf[k * rows : (k + 1) * rows, g * gw : (g + 1) * gw] = x_ref[g]
    for copy in copies:
        copy.wait()
    acc = jnp.dot(
        x_buf[...], w_buf[...].reshape(G * gw, 3 * HC), preferred_element_type=jnp.float32
    )

    def normed(h, gain):
        v = acc[:, h * HD : (h + 1) * HD]
        ms = jnp.mean(v * v, axis=-1, keepdims=True)
        return (v * lax.rsqrt(ms + 1e-06) * gain).astype(jnp.bfloat16)

    for h in range(NH):
        q_ref[:, h * HD : (h + 1) * HD] = normed(h, qg_ref[...]) * jnp.bfloat16(0.125)
        kv_ref[:, h * HD : (h + 1) * HD] = normed(NH + h, kg_ref[...])
    kv_ref[:, HC:] = acc[:, 2 * HC :].astype(jnp.bfloat16)


def attention_kernel(text_count, s_ref, qa_ref, qb_ref, *refs):
    *sources, o_ref, k_buf, v_buf = refs
    rows = o_ref.shape[1]
    step = pl.program_id(0)

    @pl.when(step == 0)
    def _():
        at = 0
        for r in sources:
            span = slice(at, at + r.shape[0])
            at += r.shape[0]
            for h in range(NH):
                k_buf[h, span] = r[:, h * HD : (h + 1) * HD]
                v_buf[h, span] = r[:, HC + h * HD : HC + (h + 1) * HD]

    keys = k_buf.shape[1]
    cut = keys - 128
    live = cut + lax.broadcasted_iota(jnp.int32, (1, 128), 1) < keys - sources[-1].shape[0] + text_count
    heads = []
    for h in range(NH):
        ks = slice(h * HD, (h + 1) * HD)
        q = jnp.where(step == 0, qa_ref[:, ks], qb_ref[:, ks])

        def scored(span):
            return lax.dot_general(
                q, k_buf[h, span], (((1,), (1,)), ((), ())), preferred_element_type=jnp.float32
            )

        head, tail = scored(slice(0, cut)), jnp.where(live, scored(slice(cut, keys)), -jnp.inf)
        top = jnp.maximum(
            jnp.max(head, axis=-1, keepdims=True), jnp.max(tail, axis=-1, keepdims=True)
        )
        head, tail = jnp.exp(head - top), jnp.exp(tail - top)
        total = jnp.sum(head, axis=-1, keepdims=True) + jnp.sum(tail, axis=-1, keepdims=True)
        probs = jnp.concatenate([head.astype(jnp.bfloat16), tail.astype(jnp.bfloat16)], axis=-1)
        mixed = jnp.dot(probs, v_buf[h], preferred_element_type=jnp.float32)
        heads.append((mixed / total).astype(jnp.bfloat16))
    out = jnp.concatenate(heads, axis=-1)
    for k in range(Y):
        y = (s_ref[0] + k) & 3
        o_ref[2 * y + (s_ref[1] ^ step)] = out[k * rows : (k + 1) * rows]


def out_kernel(fo, s_ref, h_ref, wa_ref, wb_ref, x_ref, m_ref, o_ref, h_buf, w_buf, sems):
    parts, rows, width = o_ref.shape
    own = s_ref[0]
    copies = [
        pltpu.make_async_copy(wa_ref, w_buf.at[own], sems.at[0]),
        pltpu.make_async_copy(wb_ref, w_buf.at[1 - own], sems.at[1]),
    ]
    for copy in copies:
        copy.start()
    bo = wa_ref.shape[1]
    half = 2 * Y * bo
    for p in range(parts):
        row = jnp.concatenate([h_ref[2 * y + p] for y in range(Y)], axis=-1)
        for c in range(2):
            pieces = []
            for pair in range(2 * Y):
                s = 2 * pair + c
                pieces.append(row[:, s * fo : (s + 1) * fo])
                pieces.append(jnp.zeros((rows, bo - fo), row.dtype))
            h_buf[p * rows : (p + 1) * rows, c * half : (c + 1) * half] = jnp.concatenate(
                pieces, axis=-1
            )
    for copy in copies:
        copy.wait()
    acc = jnp.dot(
        h_buf[...], w_buf[...].reshape(2 * half, width), preferred_element_type=jnp.float32
    )
    gate = m_ref[...]
    for p in range(parts):
        floats = x_ref[p].astype(jnp.float32)
        o_ref[p] = (floats + gate * acc[p * rows : (p + 1) * rows]).astype(jnp.bfloat16)


def on_device(hidden, ancestors, timestep, mod_table, w_qkv, w_out, q_gain, k_gain, text_kv):
    parts, rows, width = hidden.shape
    inner = w_out.shape[0] * 16
    fw = w_qkv.shape[0]
    bw = -(-fw // 32) * 32
    gw = Y * bw
    yi, xi, ci = (lax.axis_index(a).astype(jnp.int32) for a in ("y", "xl", "c"))
    bf16 = jnp.bfloat16
    shape = jax.ShapeDtypeStruct

    packed = pl.pallas_call(
        functools.partial(pack_kernel, fw),
        out_shape=shape((GROUPS, parts, RT, gw), bf16),
        in_specs=[whole()],
        out_specs=whole(),
        compiler_params=params(),
    )(hidden)
    chunks = lax.all_to_all(packed, GROUP, 0, 0)

    w_qkv, packed_too = lax.optimization_barrier((w_qkv, packed))
    split = pl.pallas_call(
        weight_kernel,
        out_shape=shape((Y, bw, 3 * HC), bf16),
        in_specs=[scalar(), whole()],
        out_specs=whole(),
        compiler_params=params(),
    )(yi[None], jnp.pad(w_qkv, ((0, bw - fw), (0, 0))))
    w_mine = placed_in_order(
        lambda k, s: (s[0] - k) & 3, yi[None], [split[0]] + [turn(split[k], "y", k) for k in (1, 2, 3)]
    )
    fo = w_out.shape[0]
    w_out, w_mine = lax.optimization_barrier((w_out, w_mine))
    w_across = swap(w_mine, "c")
    w_side = swap(w_mine, "xl")
    w_corner = swap(w_side, "c")
    o_near = jnp.pad(w_out, ((0, -fo % RT), (0, 0)))
    o_side = swap(o_near, "xl")
    o_pieces = [p if k == 0 else turn(p, "y", -k) for p in (o_near, o_side) for k in range(Y)]
    o_mine = placed_in_order(
        lambda k, s: 2 * ((s[0] + k) & 3) + (s[1] ^ (k >> 2)), jnp.stack([yi, xi]), o_pieces
    )
    o_across = swap(o_mine, "c")

    text_count = text_kv.shape[1]
    text_pad = -(-text_count // 128) * 128
    text = jnp.pad(text_kv, ((0, 0), (0, text_pad - text_count), (0, Y * HC - inner)))
    text = lax.dynamic_slice_in_dim(text, yi * HC, HC, axis=2)
    text = jnp.concatenate([text[0], text[1]], axis=-1)

    modulation = lax.dynamic_index_in_dim(mod_table, timestep[0], 0, keepdims=False)
    gate = modulation[2:]
    modulation = modulation[:2]
    modulation = jnp.pad(modulation.reshape(2, Y, G, fw), ((0, 0), (0, 0), (0, 0), (0, bw - fw)))
    modulation = jnp.transpose(modulation, (0, 2, 1, 3)).reshape(2, G, gw)
    live = jnp.asarray((np.arange(gw) % bw < fw)[None], jnp.float32)
    live, modulation, gate, text, chunks = lax.optimization_barrier(
        (live, modulation, gate, text, chunks)
    )

    chosen = pl.pallas_call(
        pick_kernel,
        out_shape=shape((GROUPS * parts, RT, gw), bf16),
        in_specs=[scalar(), whole()],
        out_specs=whole(),
        compiler_params=params(),
    )(ancestors, chunks.reshape(GROUPS * parts, RT, gw))
    back = lax.all_to_all(chosen.reshape(GROUPS, parts, RT, gw), GROUP, 0, 0)

    keep, send = pl.pallas_call(
        functools.partial(norm_kernel, width),
        out_shape=[shape((G, rows, gw), bf16)] * 2,
        in_specs=[scalar()] + [whole()] * 3,
        out_specs=[whole()] * 2,
        compiler_params=params(),
    )(xi[None], back, modulation, live)

    def project(mine):
        blocks = [mine] + [turn(mine, "y", -k) for k in (1, 2, 3)]
        return pl.pallas_call(
            qkv_kernel,
            in_specs=[scalar()]
            + [whole()] * 4
            + [pl.BlockSpec(memory_space=pl.ANY)] * 4
            + [whole()] * 2,
            out_specs=[whole()] * 2,
            out_shape=[shape((Y * rows, HC), bf16), shape((Y * rows, 2 * HC), bf16)],
            scratch_shapes=[
                pltpu.VMEM((Y * rows, G * gw), bf16),
                pltpu.VMEM((G, Y, bw, 3 * HC), bf16),
                pltpu.SemaphoreType.DMA((G,)),
            ],
            compiler_params=params(32),
        )(
            (xi * 2 + ci)[None],
            *blocks,
            w_mine,
            w_across,
            w_side,
            w_corner,
            q_gain[None],
            k_gain[None],
        )

    q_a, kv_a = project(keep)
    q_b, kv_b = project(swap(send, "xl"))
    picked = pl.pallas_call(
        functools.partial(restore_kernel, fw),
        out_shape=shape((parts, rows, width), bf16),
        in_specs=[whole()],
        out_specs=whole(),
        compiler_params=params(),
    )(back)
    kv_c, kv_d = swap(kv_a, "c"), swap(kv_b, "c")
    count = q_a.shape[0]
    once = lambda r, w: pl.BlockSpec((r, w), lambda i: (0, 0))
    attended = pl.pallas_call(
        functools.partial(attention_kernel, text_count),
        grid=(2,),
        in_specs=[scalar()]
        + [once(count, HC)] * 2
        + [once(count, 2 * HC)] * 4
        + [once(text_pad, 2 * HC)],
        out_specs=pl.BlockSpec((2 * Y, rows, HC), lambda i: (0, 0, 0)),
        out_shape=shape((2 * Y, rows, HC), bf16),
        scratch_shapes=[pltpu.VMEM((NH, 4 * count + text_pad, HD), bf16)] * 2,
        compiler_params=params(40),
    )(jnp.stack([yi, xi]), q_a, q_b, kv_a, kv_b, kv_c, kv_d, text)

    home = lax.all_to_all(attended, ("y", "xl"), 0, 0)
    return pl.pallas_call(
        functools.partial(out_kernel, fo),
        in_specs=[scalar(), whole()]
        + [pl.BlockSpec(memory_space=pl.ANY)] * 2
        + [whole()] * 2,
        out_specs=whole(),
        out_shape=shape((parts, rows, width), bf16),
        scratch_shapes=[
            pltpu.VMEM((parts * rows, 2 * o_mine.size // width), bf16),
            pltpu.VMEM((2,) + o_mine.shape, bf16),
            pltpu.SemaphoreType.DMA((2,)),
        ],
        compiler_params=params(32),
    )(ci[None], home, o_mine, o_across, picked, gate)


def solution(mesh):
    fine = Mesh(np.asarray(mesh.devices).reshape(SIZES), AXES)
    placed = (
        P(("xh", "z"), ("y", "xl", "c"), None),
        P(),
        P(),
        P(),
        P(("y", "xl", "c"), None),
        P(("y", "xl", "c"), None),
        P(),
        P(),
        P(),
    )
    return jax.shard_map(
        on_device,
        mesh=fine,
        in_specs=placed,
        out_specs=P(("xh", "z"), ("y", "xl", "c"), None),
        check_vma=False,
    )
```

```python
import functools

import jax
import jax.numpy as jnp
import numpy as np
from jax import lax
from jax.experimental import pallas as pl
from jax.experimental.pallas import tpu as pltpu
from jax.sharding import Mesh, PartitionSpec as P

HD = 64
AXES = ("xh", "z", "y", "xl", "c")
SIZES = (2, 8, 4, 2, 2)
GROUP = ("xh", "z")
GROUPS = 16
Y = 4
G = 4
NH = 5
HC = NH * HD
RT = 16
FIRST = ((0, 0), (0, 1), (1, 0), (3, 0))
SECOND = ((1, 1), (3, 1), (2, 0), (2, 1))


def params(mib=16):
    return pltpu.CompilerParams(vmem_limit_bytes=mib * 1024 * 1024)


def whole():
    return pl.BlockSpec(memory_space=pltpu.VMEM)


def scalar():
    return pl.BlockSpec(memory_space=pltpu.SMEM)


def swap(x, axis):
    return lax.ppermute(x, axis, [(0, 1), (1, 0)])


def turn(x, axis, by):
    n = SIZES[AXES.index(axis)]
    return lax.ppermute(x, axis, [(i, (i + by) % n) for i in range(n)])


def beside(x, by):
    n = 4
    return lax.ppermute(x, ("xh", "xl"), [(i, (i + by) % n) for i in range(n)])


def across(x, by):
    pairs = [(2 * y + l, 2 * ((y + by) % Y) + 1 - l) for y in range(Y) for l in range(2)]
    return lax.ppermute(x, ("y", "xl"), pairs)


def pack_kernel(fw, x_ref, o_ref):
    parts, rows, _ = x_ref.shape
    bw = o_ref.shape[-1] // Y
    for p in range(parts):
        for i in range(rows // RT):
            for g in range(G):
                pieces = []
                for y in range(Y):
                    lo = (y * G + g) * fw
                    pieces.append(x_ref[p, i * RT : (i + 1) * RT, lo : lo + fw])
                    pieces.append(jnp.zeros((RT, bw - fw), x_ref.dtype))
                o_ref[G * i + g, p] = jnp.concatenate(pieces, axis=-1)


def restore_kernel(fw, x_ref, o_ref):
    parts, rows, _ = o_ref.shape
    bw = x_ref.shape[-1] // Y
    for p in range(parts):
        for i in range(rows // RT):
            row = [x_ref[G * i + g, p] for g in range(G)]
            pieces = [row[g][:, y * bw : y * bw + fw] for y in range(Y) for g in range(G)]
            o_ref[p, i * RT : (i + 1) * RT, :] = jnp.concatenate(pieces, axis=-1)


def pick_kernel(a_ref, x_ref, o_ref):
    def step(p, _):
        o_ref[p] = x_ref[a_ref[p]]
        return 0

    lax.fori_loop(0, x_ref.shape[0], step, 0, unroll=4)


def norm_kernel(fw, s_ref, x_ref, m_ref, keep_ref, send_ref):
    count = keep_ref.shape[1] // RT
    bw = keep_ref.shape[-1] // Y
    width = m_ref.shape[-1]
    side = s_ref[0]
    lane = lax.broadcasted_iota(jnp.int32, (1, Y * bw), 1)
    live = jnp.zeros((1, Y * bw), jnp.float32)
    for y in range(Y):
        live = jnp.where((lane >= y * bw) & (lane < y * bw + fw), 1.0, live)

    def grouped(row):
        out = []
        for g in range(G):
            pieces = []
            for y in range(Y):
                lo = (y * G + g) * fw
                pieces += [m_ref[row : row + 1, lo : lo + fw], jnp.zeros((1, bw - fw), jnp.float32)]
            out.append(jnp.concatenate(pieces, axis=-1))
        return out

    shift, scale = grouped(0), [1.0 + r for r in grouped(1)]
    for which, o_ref in enumerate((keep_ref, send_ref)):
        for i in range(count):
            floats = [x_ref[G * i + g, side ^ which].astype(jnp.float32) for g in range(G)]
            center = sum(jnp.sum(f, axis=-1, keepdims=True) for f in floats) / width
            moved = [(f - center) * live for f in floats]
            spread = sum(jnp.sum(m * m, axis=-1, keepdims=True) for m in moved) / width
            inverse = lax.rsqrt(spread + 1e-06)
            for g in range(G):
                out = (moved[g] * inverse) * scale[g] + shift[g]
                o_ref[g, i * RT : (i + 1) * RT, :] = out.astype(jnp.bfloat16)


def weight_kernel(s_ref, w_ref, o_ref):
    inner = w_ref.shape[1] // 3
    for y in range(Y):
        at = (y - s_ref[0]) & 3
        pieces = []
        for t in range(3):
            lo, hi = y * HC, min(inner, (y + 1) * HC)
            pieces.append(w_ref[:, t * inner + lo : t * inner + hi])
            if hi - lo < HC:
                pieces.append(jnp.zeros((w_ref.shape[0], HC - hi + lo), w_ref.dtype))
        o_ref[at] = jnp.concatenate(pieces, axis=-1)


def place_kernel(order, s_ref, *refs):
    *pieces, o_ref = refs
    for k, piece in enumerate(pieces):
        o_ref[order(k, s_ref)] = piece[...]


def join_kernel(*refs):
    *pieces, o_ref = refs
    at = 0
    for piece in pieces:
        o_ref[at : at + piece.shape[0]] = piece[...]
        at += piece.shape[0]


def placed_in_order(order, scalars, pieces):
    count = len(pieces)
    return pl.pallas_call(
        functools.partial(place_kernel, order),
        out_shape=jax.ShapeDtypeStruct((count,) + pieces[0].shape, pieces[0].dtype),
        in_specs=[scalar()] + [whole()] * count,
        out_specs=whole(),
        compiler_params=params(),
    )(scalars, *pieces)


def qkv_kernel(s_ref, *refs):
    x_refs = refs[:4]
    w_ref, qg_ref, kg_ref, q_ref, kv_ref, x_buf = refs[4:]
    rows, gw = x_refs[0].shape[1:]
    for k, x_ref in enumerate(x_refs):
        for flip in range(G):
            x_buf[k * rows : (k + 1) * rows, flip * gw : (flip + 1) * gw] = x_ref[s_ref[0] ^ flip]
    acc = jnp.dot(
        x_buf[...], w_ref[...].reshape(G * gw, 3 * HC), preferred_element_type=jnp.float32
    )

    def normed(h, gain):
        v = acc[:, h * HD : (h + 1) * HD]
        ms = jnp.mean(v * v, axis=-1, keepdims=True)
        return (v * lax.rsqrt(ms + 1e-06) * gain).astype(jnp.bfloat16)

    for h in range(NH):
        q_ref[:, h * HD : (h + 1) * HD] = normed(h, qg_ref[...]) * jnp.bfloat16(0.125)
        kv_ref[:, h * HD : (h + 1) * HD] = normed(NH + h, kg_ref[...])
    kv_ref[:, HC:] = acc[:, 2 * HC :].astype(jnp.bfloat16)


def attention_kernel(text_count, s_ref, *refs):
    given, (o_ref, q_buf, kv_buf, k_buf, v_buf, sems) = refs[:7], refs[7:]
    rows = o_ref.shape[1]
    step = pl.program_id(0)

    @pl.when(step == 0)
    def _():
        copies, spans, at = [], [], 0
        for k, r in enumerate(given):
            if k < 2:
                to = q_buf.at[k]
            else:
                spans.append(slice(at, at + r.shape[0]))
                at += r.shape[0]
                to = kv_buf.at[spans[-1]]
            copies.append(pltpu.make_async_copy(r, to, sems.at[k]))
        for copy in copies:
            copy.start()
        for copy, span in zip(copies[2:], spans):
            copy.wait()
            for h in range(NH):
                k_buf[h, span] = kv_buf[span, h * HD : (h + 1) * HD]
                v_buf[h, span] = kv_buf[span, HC + h * HD : HC + (h + 1) * HD]
        for copy in copies[:2]:
            copy.wait()

    keys = k_buf.shape[1]
    cut = keys - 128
    live = cut + lax.broadcasted_iota(jnp.int32, (1, 128), 1) < keys - given[-1].shape[0] + text_count
    heads = []
    for h in range(NH):
        ks = slice(h * HD, (h + 1) * HD)
        q = q_buf[step, :, ks]

        def scored(span):
            return lax.dot_general(
                q, k_buf[h, span], (((1,), (1,)), ((), ())), preferred_element_type=jnp.float32
            )

        head, tail = scored(slice(0, cut)), jnp.where(live, scored(slice(cut, keys)), -jnp.inf)
        top = jnp.maximum(
            jnp.max(head, axis=-1, keepdims=True), jnp.max(tail, axis=-1, keepdims=True)
        )
        head, tail = jnp.exp(head - top), jnp.exp(tail - top)
        total = jnp.sum(head, axis=-1, keepdims=True) + jnp.sum(tail, axis=-1, keepdims=True)
        probs = jnp.concatenate([head.astype(jnp.bfloat16), tail.astype(jnp.bfloat16)], axis=-1)
        mixed = jnp.dot(probs, v_buf[h], preferred_element_type=jnp.float32)
        heads.append((mixed / total).astype(jnp.bfloat16))
    out = jnp.concatenate(heads, axis=-1)
    for k in range(Y):
        (turn_a, flip_a), (turn_b, flip_b) = FIRST[k], SECOND[k]
        y = (s_ref[0] + jnp.where(step == 0, turn_a, turn_b)) & 3
        side = s_ref[1] ^ jnp.where(step == 0, flip_a, flip_b)
        o_ref[2 * y + side] = out[k * rows : (k + 1) * rows]


def out_kernel(fo, s_ref, h_ref, x_ref, m_ref, *refs):
    *given, o_ref, h_buf, w_buf, sems = refs
    parts, rows, width = o_ref.shape
    count, bo, _ = w_buf.shape
    copies, filled = [], 0
    for k, r in enumerate(given):
        to = w_buf.at[filled : filled + r.shape[0]]
        filled += r.shape[0]
        copies.append(pltpu.make_async_copy(r, to, sems.at[k]))
    for copy in copies:
        copy.start()
    for p in range(parts):
        row = jnp.concatenate([h_ref[2 * y + p] for y in range(Y)], axis=-1)
        for s in range(count):
            y, x, c = s // 4, s // 2 % 2, s % 2
            at = 4 * (c ^ s_ref[2]) + ((y - s_ref[0]) & 3)
            piece = [row[:, s * fo : (s + 1) * fo], jnp.zeros((rows, bo - fo), row.dtype)]
            h_buf[2 * at + (x ^ s_ref[1]), p * rows : (p + 1) * rows, :] = jnp.concatenate(
                piece, axis=-1
            )
    features = jnp.concatenate([h_buf[k] for k in range(count)], axis=-1)
    for copy in copies:
        copy.wait()
    acc = jnp.dot(
        features, w_buf[...].reshape(count * bo, width), preferred_element_type=jnp.float32
    )
    gate = m_ref[...]
    for p in range(parts):
        floats = x_ref[p].astype(jnp.float32)
        o_ref[p] = (floats + gate * acc[p * rows : (p + 1) * rows]).astype(jnp.bfloat16)


def on_device(hidden, ancestors, timestep, mod_table, w_qkv, w_out, q_gain, k_gain, text_kv):
    parts, rows, width = hidden.shape
    inner = w_out.shape[0] * 16
    fw = w_qkv.shape[0]
    bw = -(-fw // 32) * 32
    gw = Y * bw
    yi, xi, ci = (lax.axis_index(a).astype(jnp.int32) for a in ("y", "xl", "c"))
    bf16 = jnp.bfloat16
    shape = jax.ShapeDtypeStruct

    packed = pl.pallas_call(
        functools.partial(pack_kernel, fw),
        out_shape=shape((GROUPS, parts, RT, gw), bf16),
        in_specs=[whole()],
        out_specs=whole(),
        compiler_params=params(),
    )(hidden)
    chunks = lax.all_to_all(packed, GROUP, 0, 0)

    w_qkv, w_out, packed_too = lax.optimization_barrier((w_qkv, w_out, packed))
    split = pl.pallas_call(
        weight_kernel,
        out_shape=shape((Y, bw, 3 * HC), bf16),
        in_specs=[scalar(), whole()],
        out_specs=whole(),
        compiler_params=params(),
    )(yi[None], jnp.pad(w_qkv, ((0, bw - fw), (0, 0))))
    w_pieces = [split[0]] + [turn(split[k], "y", k) for k in (1, 2, 3)]
    fo = w_out.shape[0]
    o_near = jnp.pad(w_out, ((0, -fo % RT), (0, 0)))
    o_side = swap(o_near, "xl")

    chunks, w_pieces, o_side = lax.optimization_barrier((chunks, w_pieces, o_side))
    w_mine = placed_in_order(lambda k, s: (s[0] - k) & 3, yi[None], w_pieces)

    modulation = lax.dynamic_index_in_dim(mod_table, timestep[0], 0, keepdims=False)
    gate = modulation[2:]

    chosen = pl.pallas_call(
        pick_kernel,
        out_shape=shape((GROUPS * parts, RT, gw), bf16),
        in_specs=[scalar(), whole()],
        out_specs=whole(),
        compiler_params=params(),
    )(ancestors, chunks.reshape(GROUPS * parts, RT, gw))

    chosen, w_mine, o_near, o_side = lax.optimization_barrier((chosen, w_mine, o_near, o_side))
    back = lax.all_to_all(chosen.reshape(GROUPS, parts, RT, gw), GROUP, 0, 0)
    w_sides = [beside(w_mine[: Y // 2], 1), beside(w_mine[Y // 2 :], -1)]
    w_across = swap(w_mine, "c")
    o_own = jnp.stack([o_near, o_side])
    o_next, o_last = turn(o_own, "y", -1), turn(o_own, "y", -3)

    back, w_across, o_next, o_last = lax.optimization_barrier((back, w_across, o_next, o_last))
    w_corners = [swap(piece, "c") for piece in w_sides]
    w_all = pl.pallas_call(
        join_kernel,
        out_shape=shape((G * Y, bw, 3 * HC), bf16),
        in_specs=[whole()] * 6,
        out_specs=whole(),
        compiler_params=params(),
    )(w_mine, w_across, *w_sides, *w_corners)

    keep, send = pl.pallas_call(
        functools.partial(norm_kernel, fw),
        out_shape=[shape((G, rows, gw), bf16)] * 2,
        in_specs=[scalar()] + [whole()] * 2,
        out_specs=[whole()] * 2,
        compiler_params=params(),
    )(xi[None], back, modulation)

    back, text_kv = lax.optimization_barrier((back, text_kv))
    picked = pl.pallas_call(
        functools.partial(restore_kernel, fw),
        out_shape=shape((parts, rows, width), bf16),
        in_specs=[whole()],
        out_specs=whole(),
        compiler_params=params(),
    )(back)
    text_count = text_kv.shape[1]
    text_pad = -(-text_count // 128) * 128
    text = jnp.pad(text_kv, ((0, 0), (0, text_pad - text_count), (0, Y * HC - inner)))
    text = lax.dynamic_slice_in_dim(text, yi * HC, HC, axis=2)
    text = jnp.concatenate([text[0], text[1]], axis=-1)


    other = swap(send, "xl")
    keep_1, keep_3 = turn(keep, "y", -1), turn(keep, "y", -3)
    other_1, other_3 = across(send, -1), across(send, -3)
    keep_2, other_2 = turn(keep_1, "y", -1), turn(other_3, "y", 1)

    def project(*blocks):
        return pl.pallas_call(
            qkv_kernel,
            in_specs=[scalar()] + [whole()] * 7,
            out_specs=[whole()] * 2,
            out_shape=[shape((Y * rows, HC), bf16), shape((Y * rows, 2 * HC), bf16)],
            scratch_shapes=[pltpu.VMEM((Y * rows, G * gw), bf16)],
            compiler_params=params(24),
        )((xi * 2 + ci)[None], *blocks, w_all, q_gain[None], k_gain[None])

    q_a, kv_a = project(keep, other, keep_1, keep_3)
    o_next_near, o_last_side = o_next[:1], o_last[1:]
    other_1, text, kv_a, o_next_near, o_last_side = lax.optimization_barrier(
        (other_1, text, kv_a, o_next_near, o_last_side)
    )
    q_b, kv_b = project(other_1, other_3, keep_2, other_2)
    o_own, o_next_near, o_last_side, kv_a, kv_b = lax.optimization_barrier(
        (o_own, o_next_near, o_last_side, kv_a, kv_b)
    )
    o_far = [turn(o_next_near, "y", -1), turn(o_last_side, "y", 1)]
    o_crossed = [swap(o_own, "c"), swap(o_next, "c"), None, swap(o_last, "c")]
    kv_c, kv_d = swap(kv_a, "c"), swap(kv_b, "c")
    count = q_a.shape[0]
    attended = pl.pallas_call(
        functools.partial(attention_kernel, text_count),
        grid=(2,),
        in_specs=[scalar()] + [pl.BlockSpec(memory_space=pl.ANY)] * 7,
        out_specs=pl.BlockSpec((2 * Y, rows, HC), lambda i: (0, 0, 0)),
        out_shape=shape((2 * Y, rows, HC), bf16),
        scratch_shapes=[
            pltpu.VMEM((2, count, HC), bf16),
            pltpu.VMEM((4 * count + text_pad, 2 * HC), bf16),
            pltpu.VMEM((NH, 4 * count + text_pad, HD), bf16),
            pltpu.VMEM((NH, 4 * count + text_pad, HD), bf16),
            pltpu.SemaphoreType.DMA((7,)),
        ],
        compiler_params=params(40),
    )(jnp.stack([yi, xi]), q_a, q_b, kv_a, kv_b, kv_c, kv_d, text)

    attended, o_far = lax.optimization_barrier((attended, o_far))
    o_crossed[2] = [swap(piece, "c") for piece in o_far]
    o_pieces = [o_own, o_next, *o_far, o_last, *o_crossed[:2], *o_crossed[2], o_crossed[3]]
    home = lax.all_to_all(attended, ("y", "xl"), 0, 0)
    return pl.pallas_call(
        functools.partial(out_kernel, fo),
        in_specs=[scalar()]
        + [whole()] * 3
        + [pl.BlockSpec(memory_space=pl.ANY)] * len(o_pieces),
        out_specs=whole(),
        out_shape=shape((parts, rows, width), bf16),
        scratch_shapes=[
            pltpu.VMEM((4 * Y, parts * rows, o_near.shape[0]), bf16),
            pltpu.VMEM((4 * Y,) + o_near.shape, bf16),
            pltpu.SemaphoreType.DMA((len(o_pieces),)),
        ],
        compiler_params=params(32),
    )(jnp.stack([yi, xi, ci]), home, picked, gate, *o_pieces)


def solution(mesh):
    fine = Mesh(np.asarray(mesh.devices).reshape(SIZES), AXES)
    placed = (
        P(("xh", "z"), ("y", "xl", "c"), None),
        P(),
        P(),
        P(),
        P(("y", "xl", "c"), None),
        P(("y", "xl", "c"), None),
        P(),
        P(),
        P(),
    )
    return jax.shard_map(
        on_device,
        mesh=fine,
        in_specs=placed,
        out_specs=P(("xh", "z"), ("y", "xl", "c"), None),
        check_vma=False,
    )
```

```python
import functools

import jax
import jax.numpy as jnp
import numpy as np
from jax import lax
from jax.experimental import pallas as pl
from jax.experimental.pallas import tpu as pltpu
from jax.sharding import Mesh, PartitionSpec as P

HD = 64
AXES = ("xh", "z", "y", "xl", "c")
SIZES = (2, 8, 4, 2, 2)
GROUP = ("xh", "z")
GROUPS = 16
Y = 4
G = 4
NH = 5
HC = NH * HD
RT = 16
FIRST = ((0, 0), (0, 1), (1, 0), (3, 0))
SECOND = ((1, 1), (3, 1), (2, 0), (2, 1))


def params(mib=16):
    return pltpu.CompilerParams(vmem_limit_bytes=mib * 1024 * 1024)


def whole():
    return pl.BlockSpec(memory_space=pltpu.VMEM)


def scalar():
    return pl.BlockSpec(memory_space=pltpu.SMEM)


def swap(x, axis):
    return lax.ppermute(x, axis, [(0, 1), (1, 0)])


def turn(x, axis, by):
    n = SIZES[AXES.index(axis)]
    return lax.ppermute(x, axis, [(i, (i + by) % n) for i in range(n)])


def beside(x, by):
    n = 4
    return lax.ppermute(x, ("xh", "xl"), [(i, (i + by) % n) for i in range(n)])


def across(x, by):
    pairs = [(2 * y + l, 2 * ((y + by) % Y) + 1 - l) for y in range(Y) for l in range(2)]
    return lax.ppermute(x, ("y", "xl"), pairs)


def pack_kernel(fw, x_ref, o_ref):
    parts, rows, _ = x_ref.shape
    bw = o_ref.shape[-1] // Y
    for p in range(parts):
        for i in range(rows // RT):
            for g in range(G):
                pieces = []
                for y in range(Y):
                    lo = (y * G + g) * fw
                    pieces.append(x_ref[p, i * RT : (i + 1) * RT, lo : lo + fw])
                    pieces.append(jnp.zeros((RT, bw - fw), x_ref.dtype))
                o_ref[G * i + g, p] = jnp.concatenate(pieces, axis=-1)


def restore_kernel(fw, x_ref, o_ref):
    parts, rows, _ = o_ref.shape
    bw = x_ref.shape[-1] // Y
    for p in range(parts):
        for i in range(rows // RT):
            row = [x_ref[G * i + g, p] for g in range(G)]
            pieces = [row[g][:, y * bw : y * bw + fw] for y in range(Y) for g in range(G)]
            o_ref[p, i * RT : (i + 1) * RT, :] = jnp.concatenate(pieces, axis=-1)


def pick_kernel(a_ref, x_ref, o_ref):
    def step(p, _):
        o_ref[p] = x_ref[a_ref[p]]
        return 0

    lax.fori_loop(0, x_ref.shape[0], step, 0, unroll=4)


def norm_kernel(fw, s_ref, x_ref, m_ref, keep_ref, send_ref):
    count = keep_ref.shape[1] // RT
    bw = keep_ref.shape[-1] // Y
    width = m_ref.shape[-1]
    side = s_ref[0]
    lane = lax.broadcasted_iota(jnp.int32, (1, Y * bw), 1)
    live = jnp.zeros((1, Y * bw), jnp.float32)
    for y in range(Y):
        live = jnp.where((lane >= y * bw) & (lane < y * bw + fw), 1.0, live)

    def grouped(row):
        out = []
        for g in range(G):
            pieces = []
            for y in range(Y):
                lo = (y * G + g) * fw
                pieces += [m_ref[row : row + 1, lo : lo + fw], jnp.zeros((1, bw - fw), jnp.float32)]
            out.append(jnp.concatenate(pieces, axis=-1))
        return out

    shift, scale = grouped(0), [1.0 + r for r in grouped(1)]
    for which, o_ref in enumerate((keep_ref, send_ref)):
        for i in range(count):
            floats = [x_ref[G * i + g, side ^ which].astype(jnp.float32) for g in range(G)]
            center = sum(jnp.sum(f, axis=-1, keepdims=True) for f in floats) / width
            moved = [(f - center) * live for f in floats]
            spread = sum(jnp.sum(m * m, axis=-1, keepdims=True) for m in moved) / width
            inverse = lax.rsqrt(spread + 1e-06)
            for g in range(G):
                out = (moved[g] * inverse) * scale[g] + shift[g]
                o_ref[g, i * RT : (i + 1) * RT, :] = out.astype(jnp.bfloat16)


def weight_kernel(s_ref, w_ref, o_ref):
    inner = w_ref.shape[1] // 3
    for y in range(Y):
        at = (y - s_ref[0]) & 3
        pieces = []
        for t in range(3):
            lo, hi = y * HC, min(inner, (y + 1) * HC)
            pieces.append(w_ref[:, t * inner + lo : t * inner + hi])
            if hi - lo < HC:
                pieces.append(jnp.zeros((w_ref.shape[0], HC - hi + lo), w_ref.dtype))
        o_ref[at] = jnp.concatenate(pieces, axis=-1)


def place_kernel(order, s_ref, *refs):
    *pieces, o_ref = refs
    for k, piece in enumerate(pieces):
        o_ref[order(k, s_ref)] = piece[...]


def join_kernel(*refs):
    *pieces, o_ref = refs
    at = 0
    for piece in pieces:
        o_ref[at : at + piece.shape[0]] = piece[...]
        at += piece.shape[0]


def placed_in_order(order, scalars, pieces):
    count = len(pieces)
    return pl.pallas_call(
        functools.partial(place_kernel, order),
        out_shape=jax.ShapeDtypeStruct((count,) + pieces[0].shape, pieces[0].dtype),
        in_specs=[scalar()] + [whole()] * count,
        out_specs=whole(),
        compiler_params=params(),
    )(scalars, *pieces)


def qkv_kernel(s_ref, *refs):
    x_refs = refs[:4]
    w_ref, qg_ref, kg_ref, q_ref, kv_ref, x_buf = refs[4:]
    rows, gw = x_refs[0].shape[1:]
    for k, x_ref in enumerate(x_refs):
        for flip in range(G):
            x_buf[k * rows : (k + 1) * rows, flip * gw : (flip + 1) * gw] = x_ref[s_ref[0] ^ flip]
    acc = jnp.dot(
        x_buf[...], w_ref[...].reshape(G * gw, 3 * HC), preferred_element_type=jnp.float32
    )

    def normed(h, gain):
        v = acc[:, h * HD : (h + 1) * HD]
        ms = jnp.mean(v * v, axis=-1, keepdims=True)
        return (v * lax.rsqrt(ms + 1e-06) * gain).astype(jnp.bfloat16)

    for h in range(NH):
        q_ref[:, h * HD : (h + 1) * HD] = normed(h, qg_ref[...]) * jnp.bfloat16(0.125)
        kv_ref[:, h * HD : (h + 1) * HD] = normed(NH + h, kg_ref[...])
    kv_ref[:, HC:] = acc[:, 2 * HC :].astype(jnp.bfloat16)


def attention_kernel(text_count, s_ref, *refs):
    given, (o_ref, q_buf, kv_buf, k_buf, v_buf, sems) = refs[:7], refs[7:]
    rows = o_ref.shape[1]
    step = pl.program_id(0)

    @pl.when(step == 0)
    def _():
        copies, spans, at = [], [], 0
        for k, r in enumerate(given):
            if k < 2:
                to = q_buf.at[k]
            else:
                spans.append(slice(at, at + r.shape[0]))
                at += r.shape[0]
                to = kv_buf.at[spans[-1]]
            copies.append(pltpu.make_async_copy(r, to, sems.at[k]))
        for copy in copies:
            copy.start()
        for copy, span in zip(copies[2:], spans):
            copy.wait()
            for h in range(NH):
                k_buf[h, span] = kv_buf[span, h * HD : (h + 1) * HD]
                v_buf[h, span] = kv_buf[span, HC + h * HD : HC + (h + 1) * HD]
        for copy in copies[:2]:
            copy.wait()

    keys = k_buf.shape[1]
    cut = keys - 128
    live = cut + lax.broadcasted_iota(jnp.int32, (1, 128), 1) < keys - given[-1].shape[0] + text_count
    heads = []
    for h in range(NH):
        ks = slice(h * HD, (h + 1) * HD)
        q = q_buf[step, :, ks]

        def scored(span):
            return lax.dot_general(
                q, k_buf[h, span], (((1,), (1,)), ((), ())), preferred_element_type=jnp.float32
            )

        head, tail = scored(slice(0, cut)), jnp.where(live, scored(slice(cut, keys)), -jnp.inf)
        top = jnp.maximum(
            jnp.max(head, axis=-1, keepdims=True), jnp.max(tail, axis=-1, keepdims=True)
        )
        head, tail = jnp.exp(head - top), jnp.exp(tail - top)
        total = jnp.sum(head, axis=-1, keepdims=True) + jnp.sum(tail, axis=-1, keepdims=True)
        probs = jnp.concatenate([head.astype(jnp.bfloat16), tail.astype(jnp.bfloat16)], axis=-1)
        mixed = jnp.dot(probs, v_buf[h], preferred_element_type=jnp.float32)
        heads.append((mixed / total).astype(jnp.bfloat16))
    out = jnp.concatenate(heads, axis=-1)
    for k in range(Y):
        (turn_a, flip_a), (turn_b, flip_b) = FIRST[k], SECOND[k]
        y = (s_ref[0] + jnp.where(step == 0, turn_a, turn_b)) & 3
        side = s_ref[1] ^ jnp.where(step == 0, flip_a, flip_b)
        o_ref[2 * y + side] = out[k * rows : (k + 1) * rows]


def out_kernel(fo, s_ref, h_ref, x_ref, m_ref, *refs):
    *given, o_ref, h_buf, w_buf, sems = refs
    parts, rows, width = o_ref.shape
    count, bo, _ = w_buf.shape
    copies, filled = [], 0
    for k, r in enumerate(given):
        to = w_buf.at[filled : filled + r.shape[0]]
        filled += r.shape[0]
        copies.append(pltpu.make_async_copy(r, to, sems.at[k]))
    for copy in copies:
        copy.start()
    for p in range(parts):
        row = jnp.concatenate([h_ref[2 * y + p] for y in range(Y)], axis=-1)
        for s in range(count):
            y, x, c = s // 4, s // 2 % 2, s % 2
            at = 4 * (c ^ s_ref[2]) + ((y - s_ref[0]) & 3)
            piece = [row[:, s * fo : (s + 1) * fo], jnp.zeros((rows, bo - fo), row.dtype)]
            h_buf[2 * at + (x ^ s_ref[1]), p * rows : (p + 1) * rows, :] = jnp.concatenate(
                piece, axis=-1
            )
    features = jnp.concatenate([h_buf[k] for k in range(count)], axis=-1)
    for copy in copies:
        copy.wait()
    acc = jnp.dot(
        features, w_buf[...].reshape(count * bo, width), preferred_element_type=jnp.float32
    )
    gate = m_ref[...]
    for p in range(parts):
        floats = x_ref[p].astype(jnp.float32)
        o_ref[p] = (floats + gate * acc[p * rows : (p + 1) * rows]).astype(jnp.bfloat16)


def on_device(hidden, ancestors, timestep, mod_table, w_qkv, w_out, q_gain, k_gain, text_kv):
    parts, rows, width = hidden.shape
    inner = w_out.shape[0] * 16
    fw = w_qkv.shape[0]
    bw = -(-fw // 32) * 32
    gw = Y * bw
    yi, xi, ci = (lax.axis_index(a).astype(jnp.int32) for a in ("y", "xl", "c"))
    bf16 = jnp.bfloat16
    shape = jax.ShapeDtypeStruct

    packed = pl.pallas_call(
        functools.partial(pack_kernel, fw),
        out_shape=shape((GROUPS, parts, RT, gw), bf16),
        in_specs=[whole()],
        out_specs=whole(),
        compiler_params=params(),
    )(hidden)
    chunks = lax.all_to_all(packed, GROUP, 0, 0)

    w_qkv, w_out, packed_too = lax.optimization_barrier((w_qkv, w_out, packed))
    split = pl.pallas_call(
        weight_kernel,
        out_shape=shape((Y, bw, 3 * HC), bf16),
        in_specs=[scalar(), whole()],
        out_specs=whole(),
        compiler_params=params(),
    )(yi[None], jnp.pad(w_qkv, ((0, bw - fw), (0, 0))))
    w_pieces = [split[0]] + [turn(split[k], "y", k) for k in (1, 2, 3)]
    fo = w_out.shape[0]
    o_near = jnp.pad(w_out, ((0, -fo % RT), (0, 0)))
    o_side = swap(o_near, "xl")

    text_count = text_kv.shape[1]
    text_pad = -(-text_count // 128) * 128
    text = jnp.pad(text_kv, ((0, 0), (0, text_pad - text_count), (0, Y * HC - inner)))
    text = lax.dynamic_slice_in_dim(text, yi * HC, HC, axis=2)
    text = jnp.concatenate([text[0], text[1]], axis=-1)

    chunks, w_pieces, o_side, text = lax.optimization_barrier((chunks, w_pieces, o_side, text))
    w_mine = placed_in_order(lambda k, s: (s[0] - k) & 3, yi[None], w_pieces)

    modulation = lax.dynamic_index_in_dim(mod_table, timestep[0], 0, keepdims=False)
    gate = modulation[2:]

    chosen = pl.pallas_call(
        pick_kernel,
        out_shape=shape((GROUPS * parts, RT, gw), bf16),
        in_specs=[scalar(), whole()],
        out_specs=whole(),
        compiler_params=params(),
    )(ancestors, chunks.reshape(GROUPS * parts, RT, gw))

    chosen, w_mine, o_near, o_side = lax.optimization_barrier((chosen, w_mine, o_near, o_side))
    back = lax.all_to_all(chosen.reshape(GROUPS, parts, RT, gw), GROUP, 0, 0)
    w_sides = [beside(w_mine[: Y // 2], 1), beside(w_mine[Y // 2 :], -1)]
    w_across = swap(w_mine, "c")
    o_own = jnp.stack([o_near, o_side])
    o_next, o_last = turn(o_own, "y", -1), turn(o_own, "y", -3)

    back, w_across, o_next, o_last = lax.optimization_barrier((back, w_across, o_next, o_last))
    w_corners = [swap(piece, "c") for piece in w_sides]
    w_all = pl.pallas_call(
        join_kernel,
        out_shape=shape((G * Y, bw, 3 * HC), bf16),
        in_specs=[whole()] * 6,
        out_specs=whole(),
        compiler_params=params(),
    )(w_mine, w_across, *w_sides, *w_corners)

    keep, send = pl.pallas_call(
        functools.partial(norm_kernel, fw),
        out_shape=[shape((G, rows, gw), bf16)] * 2,
        in_specs=[scalar()] + [whole()] * 2,
        out_specs=[whole()] * 2,
        compiler_params=params(),
    )(xi[None], back, modulation)

    picked = pl.pallas_call(
        functools.partial(restore_kernel, fw),
        out_shape=shape((parts, rows, width), bf16),
        in_specs=[whole()],
        out_specs=whole(),
        compiler_params=params(),
    )(back)
    other = swap(send, "xl")
    keep_1, keep_3 = turn(keep, "y", -1), turn(keep, "y", -3)
    other_1, other_3 = across(send, -1), across(send, -3)
    keep_2, other_2 = turn(keep_1, "y", -1), turn(other_3, "y", 1)

    def project(*blocks):
        return pl.pallas_call(
            qkv_kernel,
            in_specs=[scalar()] + [whole()] * 7,
            out_specs=[whole()] * 2,
            out_shape=[shape((Y * rows, HC), bf16), shape((Y * rows, 2 * HC), bf16)],
            scratch_shapes=[pltpu.VMEM((Y * rows, G * gw), bf16)],
            compiler_params=params(24),
        )((xi * 2 + ci)[None], *blocks, w_all, q_gain[None], k_gain[None])

    q_a, kv_a = project(keep, other, keep_1, keep_3)
    o_next_near, o_last_side = o_next[:1], o_last[1:]
    other_1, kv_a, o_next_near, o_last_side = lax.optimization_barrier(
        (other_1, kv_a, o_next_near, o_last_side)
    )
    q_b, kv_b = project(other_1, other_3, keep_2, other_2)
    o_own, o_next_near, o_last_side, kv_a, kv_b = lax.optimization_barrier(
        (o_own, o_next_near, o_last_side, kv_a, kv_b)
    )
    o_far = [turn(o_next_near, "y", -1), turn(o_last_side, "y", 1)]
    o_crossed = [swap(o_own, "c"), swap(o_next, "c"), None, swap(o_last, "c")]
    kv_c, kv_d = swap(kv_a, "c"), swap(kv_b, "c")
    count = q_a.shape[0]
    attended = pl.pallas_call(
        functools.partial(attention_kernel, text_count),
        grid=(2,),
        in_specs=[scalar()] + [pl.BlockSpec(memory_space=pl.ANY)] * 7,
        out_specs=pl.BlockSpec((2 * Y, rows, HC), lambda i: (0, 0, 0)),
        out_shape=shape((2 * Y, rows, HC), bf16),
        scratch_shapes=[
            pltpu.VMEM((2, count, HC), bf16),
            pltpu.VMEM((4 * count + text_pad, 2 * HC), bf16),
            pltpu.VMEM((NH, 4 * count + text_pad, HD), bf16),
            pltpu.VMEM((NH, 4 * count + text_pad, HD), bf16),
            pltpu.SemaphoreType.DMA((7,)),
        ],
        compiler_params=params(40),
    )(jnp.stack([yi, xi]), q_a, q_b, kv_a, kv_b, kv_c, kv_d, text)

    attended, o_far = lax.optimization_barrier((attended, o_far))
    o_crossed[2] = [swap(piece, "c") for piece in o_far]
    o_pieces = [o_own, o_next, *o_far, o_last, *o_crossed[:2], *o_crossed[2], o_crossed[3]]
    home = lax.all_to_all(attended, ("y", "xl"), 0, 0)
    return pl.pallas_call(
        functools.partial(out_kernel, fo),
        in_specs=[scalar()]
        + [whole()] * 3
        + [pl.BlockSpec(memory_space=pl.ANY)] * len(o_pieces),
        out_specs=whole(),
        out_shape=shape((parts, rows, width), bf16),
        scratch_shapes=[
            pltpu.VMEM((4 * Y, parts * rows, o_near.shape[0]), bf16),
            pltpu.VMEM((4 * Y,) + o_near.shape, bf16),
            pltpu.SemaphoreType.DMA((len(o_pieces),)),
        ],
        compiler_params=params(32),
    )(jnp.stack([yi, xi, ci]), home, picked, gate, *o_pieces)


def solution(mesh):
    fine = Mesh(np.asarray(mesh.devices).reshape(SIZES), AXES)
    placed = (
        P(("xh", "z"), ("y", "xl", "c"), None),
        P(),
        P(),
        P(),
        P(("y", "xl", "c"), None),
        P(("y", "xl", "c"), None),
        P(),
        P(),
        P(),
    )
    return jax.shard_map(
        on_device,
        mesh=fine,
        in_specs=placed,
        out_specs=P(("xh", "z"), ("y", "xl", "c"), None),
        check_vma=False,
    )
```
